512 devices in a mesh: dp: 128 (over x, z_hi, y), code: 4 (over z_lo, core).
Axes of the slice: x: 4, y: 8, z: 8 (z_hi: 4, z_lo: 2; z = z_hi * 2 + z_lo), core: 2. Of those that a mesh axis runs over, the one named last changes fastest.
Arguments:
- grad_parts: bfloat16 [128, 4, 128, 6144], P('dp', 'code'), may hold values from -2.5 to 2.5
- params: float32 [4, 128, 6144], P('code', 'dp'), may hold values from -6 to 6
- moment: float32 [4, 128, 6144], P('code', 'dp'), may hold values from -2 to 2
- variance: float32 [4, 128, 6144], P('code', 'dp'), may hold values from 0.001 to 2
- holders: int32 [128, 2], P('dp'), may hold values from 0 to 3, as said below
- nodes: int32 [6], replicated, may hold values from 1 to 16, as said below
Outputs:
- new_params: float32 [4, 128, 6144], P('code', 'dp')
- new_moment: float32 [4, 128, 6144], P('code', 'dp')
- new_variance: float32 [4, 128, 6144], P('code', 'dp')
- parity_store: float32 [4, 128, 3, 6144], P('code', 'dp')
The draws below stay inside these ranges and needn't reach their ends.
Inputs may be any that keep to these rules, and one draw needn't show every extreme that they name: `holders`: the two entries of a row are different members. All 6 nodes are different.
All inputs are finite; a program needn't handle non-finite values.
Results may differ from the reference program's by a relative error of at most 0.0003.
Values may be sent and summed in bfloat16 or wider, within the bound.
No kernel may reach another device: no remote copies, remote signals or barrier semaphores. Data moves between devices by JAX's collectives and lax.ppermute only.
A program may use at most 64 MiB of HBM per device.

```python
import math
import jax
import jax.numpy as jnp
from jax import lax

SHARD = 6144
GROUPS = 128
CODERS = 4


def draw_holders(key, part):
    key = jax.random.fold_in(key, 11)
    row_keys = jax.random.split(key, GROUPS)
    orders = jax.vmap(lambda row_key: jax.random.permutation(row_key, CODERS))(row_keys)
    return orders[:, :2].astype(jnp.int32)


def draw_nodes(key, part):
    key = jax.random.fold_in(key, 23)
    order = jax.random.permutation(key, 16)
    return (order[:2 + CODERS] + 1).astype(jnp.int32)


def raised(drawn, rng, source, target, shards_of, factor):
    owner, partner = [(jnp.arange(drawn.shape[dim]) // (drawn.shape[dim] // shards_of)).reshape([-1 if axis == dim else 1 for axis in range(drawn.ndim)]) for dim in (source, target)]
    chosen = jax.random.permutation(rng, shards_of)[partner]
    strong = (owner == chosen) | (owner == (partner + shards_of // 2) % shards_of)
    return jnp.where(strong, factor * drawn, drawn)


def shard_levels(key, shape, cuts, smallest, largest):
    def one(axis_at, blocks):
        heights = jax.random.uniform(jax.random.fold_in(jax.random.fold_in(key, 6), axis_at), (blocks,), jnp.float32, smallest / len(cuts), largest / len(cuts))
        return jnp.repeat(jnp.exp(heights), shape[axis_at] // blocks).reshape((-1,) + (1,) * (len(shape) - axis_at - 1))

    level = one(*cuts[0])
    for cut in cuts[1:]:
        level = level * one(*cut)
    return level


def normal_values(rng, dims, scale, bound, shards=(), kind=jnp.bfloat16):
    values = jax.random.normal(rng, dims, jnp.float32) * scale
    if len(shards) > 0:
        values = shard_levels(rng, dims, shards, -0.22, 0.18) * values
    return jnp.clip(values, min=-bound, max=bound).astype(kind)


def gaussian_with(key, dims, scale, reach, pieces, heavy, held_as=jnp.bfloat16):
    drawn = scale * jax.random.normal(key, dims, jnp.float32)
    if pieces:
        drawn = drawn * shard_levels(key, dims, pieces, -0.22, 0.18)
    return jnp.clip(raised(drawn, jax.random.fold_in(key, 3), *heavy), -reach, reach).astype(held_as)


def setup_inputs(seed: int = 0) -> dict:
    keys = jax.random.split(jax.random.key(seed), 7)
    return {
        "grad_parts": gaussian_with(keys[0], (GROUPS, CODERS, GROUPS, SHARD), 0.1, 2.5, ((0, 128), (1, 4)), (0, 2, 128, 5.5)),
        "params": normal_values(keys[1], (CODERS, GROUPS, SHARD), 1.0, 6.0, ((0, 4), (1, 128)), jnp.float32),
        "moment": normal_values(keys[2], (CODERS, GROUPS, SHARD), 0.3, 2.0, ((0, 4), (1, 128)), jnp.float32),
        "variance": jnp.clip(jnp.exp(math.log(2.0) - 7.6009024 * jax.random.uniform(keys[3], (CODERS, GROUPS, SHARD), jnp.float32) ** shard_levels(keys[3], (CODERS, GROUPS, SHARD), ((0, 4), (1, 128)), -0.2, 0.2)), 0.001, 2.0),
        "holders": draw_holders(jax.random.fold_in(keys[6], 71), 0),
        "nodes": draw_nodes(jax.random.fold_in(keys[6], 71), 0),
    }


beta_one = 0.9
beta_two = 0.95
learn_rate = 0.02
decay_rate = 0.1
epsilon = 1e-08
bias_one = 1.0 - 0.9 ** 60
bias_two = 1.0 - 0.95 ** 60

def reference(grad_parts, params, moment, variance, holders, nodes):

    def accumulate(index, total):
        piece = lax.dynamic_index_in_dim(grad_parts, index, 0, keepdims=False)
        return total + piece.astype(jnp.float32)
    gradient = lax.fori_loop(0, GROUPS, accumulate, jnp.zeros(params.shape, jnp.float32))
    new_moment = beta_one * moment + (1.0 - beta_one) * gradient
    new_variance = beta_two * variance + (1.0 - beta_two) * gradient * gradient
    update = new_moment / bias_one / (jnp.sqrt(new_variance / bias_two) + epsilon) + decay_rate * params
    new_params = params - learn_rate * update
    states = jnp.stack([new_params, new_moment, new_variance], axis=2)
    node_values = nodes.astype(jnp.float32)
    coefficients = 4.0 / (node_values[:2][:, None] + node_values[2:][None, :])
    parity = jnp.einsum('ji,igts->jgts', coefficients, states, precision=lax.Precision.HIGHEST)
    members = jnp.arange(CODERS, dtype=jnp.int32)
    onehot = (holders[:, :, None] == members[None, None, :]).astype(jnp.float32)
    parity_store = jnp.einsum('gjc,jgts->cgts', onehot, parity, precision=lax.Precision.HIGHEST)
    return (new_params, new_moment, new_variance, parity_store)
```

```python
import jax
import jax.numpy as jnp
from jax import lax
from jax.experimental import pallas as pl
from jax.experimental.pallas import tpu as pltpu
from jax.sharding import Mesh, PartitionSpec as P

beta_one = 0.9
beta_two = 0.95
learn_rate = 0.02
decay_rate = 0.1
epsilon = 1e-08
bias_one = 1.0 - 0.9**60
bias_two = 1.0 - 0.95**60

DP = ("x", "zh", "yh", "yl")
LANES = 128


def parity_kernel(holders_ref, nodes_ref, states_ref, out_ref):
    member = lax.axis_index("code")
    own = [jnp.where(holders_ref[0, j] == member, 1.0, 0.0) for j in range(2)]
    total = None
    for i in range(states_ref.shape[0]):
        data_node = nodes_ref[2 + i].astype(jnp.float32)
        weight = jnp.zeros((1, LANES), jnp.float32)
        for j in range(2):
            node = nodes_ref[j].astype(jnp.float32)
            weight += own[j] * (4.0 / jnp.full((1, LANES), node + data_node, jnp.float32))
        term = weight * states_ref[i]
        total = term if total is None else total + term
    out_ref[...] = total


def local(grad_parts, params, moment, variance, holders, nodes):
    width = params.shape[2]
    rows = width // LANES
    x, pair = lax.axis_size("x"), lax.axis_size("yl")
    rest = lax.axis_size("zh") * lax.axis_size("yh")

    parts = grad_parts.reshape(x, rest, pair, rows, LANES).transpose(0, 2, 1, 3, 4)
    parts = parts.reshape(x * pair, rest, rows, LANES)
    parts = lax.all_to_all(parts, ("x", "yl"), 0, 0, tiled=True)
    summed = jnp.sum(parts.astype(jnp.float32), axis=0)
    summed = lax.all_to_all(summed, ("zh", "yh"), 0, 0, tiled=True)
    gradient = jnp.sum(summed, axis=0)

    params = params.reshape(rows, LANES)
    new_moment = beta_one * moment.reshape(rows, LANES) + (1.0 - beta_one) * gradient
    new_variance = (
        beta_two * variance.reshape(rows, LANES) + (1.0 - beta_two) * gradient * gradient
    )
    update = (
        new_moment / bias_one / (jnp.sqrt(new_variance / bias_two) + epsilon) + decay_rate * params
    )
    new_params = params - learn_rate * update

    states = jnp.concatenate([new_params, new_moment, new_variance], axis=0)
    states = lax.all_gather(states, "code", axis=0, tiled=False)
    parity = pl.pallas_call(
        parity_kernel,
        out_shape=jax.ShapeDtypeStruct((3 * rows, LANES), jnp.float32),
        in_specs=[pl.BlockSpec(memory_space=pltpu.SMEM)] * 2
        + [pl.BlockSpec(memory_space=pltpu.VMEM)],
        out_specs=pl.BlockSpec(memory_space=pltpu.VMEM),
    )(holders, nodes, states)
    return (
        new_params.reshape(1, 1, width),
        new_moment.reshape(1, 1, width),
        new_variance.reshape(1, 1, width),
        parity.reshape(1, 1, 3, width),
    )


def solution(mesh):
    fine = Mesh(mesh.devices.reshape(4, 4, 4, 2, mesh.shape["code"]), DP + ("code",))
    return jax.shard_map(
        local,
        mesh=fine,
        in_specs=(
            P(DP, "code", None, None),
            P("code", DP, None),
            P("code", DP, None),
            P("code", DP, None),
            P(DP, None),
            P(),
        ),
        out_specs=(
            P("code", DP, None),
            P("code", DP, None),
            P("code", DP, None),
            P("code", DP, None, None),
        ),
        check_vma=False,
    )
```

```python
import jax
import jax.numpy as jnp
from jax import lax
from jax.experimental import pallas as pl
from jax.experimental.pallas import tpu as pltpu
from jax.sharding import Mesh, PartitionSpec as P

beta_one = 0.9
beta_two = 0.95
learn_rate = 0.02
decay_rate = 0.1
epsilon = 1e-08
bias_one = 1.0 - 0.9**60
bias_two = 1.0 - 0.95**60

X, Z, Y = 4, 4, 8
DP = ("xh", "xl", "zh", "yh", "yl")
CODE = ("zl", "core")
LANES = 128
SCALE = 4096.0


def pairs(size, shifted):
    return [((2 * k + 2 * shifted) % size, 2 * k + 1) for k in range(size // 2)]


def near_groups():
    groups = []
    for z in range(Z):
        for zl in range(2):
            for core in range(2):
                for along_x in pairs(X, core):
                    for along_y in pairs(Y, core):
                        groups.append(
                            [
                                (((x * Z + z) * Y + y) * 2 + zl) * 2 + core
                                for x in along_x
                                for y in along_y
                            ]
                        )
    return groups


def finish_kernel(
    holders_ref, nodes_ref, own_ref, states_ref, params_ref, moment_ref, variance_ref, parity_ref,
    total_ref, sems,
):
    rows = params_ref.shape[0]
    copies = [
        pltpu.make_async_copy(own_ref.at[pl.ds(rows * k, rows)], out_ref, sems.at[k])
        for k, out_ref in enumerate((params_ref, moment_ref, variance_ref))
    ]
    for copy in copies:
        copy.start()
    member = lax.axis_index(CODE)
    held = [jnp.where(holders_ref[0, j] == member, 1.0, 0.0) for j in range(2)]
    total = None
    for i in range(states_ref.shape[0]):
        data_node = nodes_ref[2 + i].astype(jnp.float32)
        weight = jnp.zeros((1, LANES), jnp.float32)
        for j in range(2):
            node = nodes_ref[j].astype(jnp.float32)
            weight += held[j] * (4.0 / jnp.full((1, LANES), node + data_node, jnp.float32))
        term = weight * states_ref[i]
        total = term if total is None else total + term
    total_ref[...] = total
    copies.append(pltpu.make_async_copy(total_ref, parity_ref, sems.at[3]))
    copies[3].start()
    for copy in copies:
        copy.wait()


def local(grad_parts, params, moment, variance, holders, nodes):
    width = params.shape[2]
    rows = width // LANES

    parts = grad_parts.reshape(X // 2, 2, Z, Y // 2, 2, rows, LANES)
    parts = parts.transpose(1, 4, 0, 2, 3, 5, 6).reshape(4, X * Z * Y // 4, rows, LANES)
    parts = lax.all_to_all(
        parts, DP + CODE, 0, 0, tiled=True, axis_index_groups=near_groups()
    )
    summed = jnp.sum(parts.astype(jnp.float32), axis=0)
    summed = (summed * SCALE).astype(jnp.float16)
    summed = lax.all_to_all(summed, ("xh", "zh", "yh"), 0, 0, tiled=True)
    gradient = jnp.sum(summed.astype(jnp.float32), axis=0) * (1.0 / SCALE)

    gradient, params, moment, variance = lax.optimization_barrier(
        (
            gradient,
            params.reshape(rows, LANES),
            moment.reshape(rows, LANES),
            variance.reshape(rows, LANES),
        )
    )
    new_moment = beta_one * moment + (1.0 - beta_one) * gradient
    new_variance = beta_two * variance + (1.0 - beta_two) * gradient * gradient
    update = (
        new_moment / bias_one / (jnp.sqrt(new_variance / bias_two) + epsilon) + decay_rate * params
    )
    new_params = params - learn_rate * update

    own = jnp.concatenate([new_params, new_moment, new_variance], axis=0)
    states = lax.all_gather(own, CODE, axis=0, tiled=False)
    state = jax.ShapeDtypeStruct((rows, LANES), jnp.float32)
    new_params, new_moment, new_variance, parity = pl.pallas_call(
        finish_kernel,
        out_shape=(state, state, state, jax.ShapeDtypeStruct((3 * rows, LANES), jnp.float32)),
        in_specs=[pl.BlockSpec(memory_space=pltpu.SMEM)] * 2
        + [pl.BlockSpec(memory_space=pltpu.VMEM)] * 2,
        out_specs=(pl.BlockSpec(memory_space=pl.ANY),) * 4,
        scratch_shapes=[
            pltpu.VMEM((3 * rows, LANES), jnp.float32),
            pltpu.SemaphoreType.DMA((4,)),
        ],
        compiler_params=pltpu.CompilerParams(vmem_limit_bytes=4 << 20),
    )(holders, nodes, own, states)
    return (
        new_params.reshape(1, 1, width),
        new_moment.reshape(1, 1, width),
        new_variance.reshape(1, 1, width),
        parity.reshape(1, 1, 3, width),
    )


def solution(mesh):
    fine = Mesh(mesh.devices.reshape(X // 2, 2, Z, Y // 2, 2, 2, 2), DP + CODE)
    return jax.shard_map(
        local,
        mesh=fine,
        in_specs=(
            P(DP, CODE, None, None),
            P(CODE, DP, None),
            P(CODE, DP, None),
            P(CODE, DP, None),
            P(DP, None),
            P(),
        ),
        out_specs=(
            P(CODE, DP, None),
            P(CODE, DP, None),
            P(CODE, DP, None),
            P(CODE, DP, None, None),
        ),
        check_vma=False,
    )
```

```python
import jax
import jax.numpy as jnp
from jax import lax
from jax.experimental import pallas as pl
from jax.experimental.pallas import tpu as pltpu
from jax.sharding import Mesh, PartitionSpec as P

beta_one = 0.9
beta_two = 0.95
learn_rate = 0.02
decay_rate = 0.1
epsilon = 1e-08
bias_one = 1.0 - 0.9**60
bias_two = 1.0 - 0.95**60

X, Z, Y = 4, 4, 8
DP = ("xh", "xl", "zh", "yh", "yl")
CODE = ("zl", "core")
LANES = 128
SCALE = 4096.0


def pairs(size, shifted):
    return [((2 * k + 2 * shifted) % size, 2 * k + 1) for k in range(size // 2)]


def near_groups():
    groups = []
    for z in range(Z):
        for zl in range(2):
            for core in range(2):
                for along_x in pairs(X, core):
                    for along_y in pairs(Y, core):
                        groups.append(
                            [
                                (((x * Z + z) * Y + y) * 2 + zl) * 2 + core
                                for x in along_x
                                for y in along_y
                            ]
                        )
    return groups


def far_groups():
    groups = []
    for xl in range(2):
        for yl in range(2):
            for zl in range(2):
                for core in range(2):
                    groups.append(
                        [
                            (((x * Z + z) * Y + y) * 2 + zl) * 2 + core
                            for x in (2 + xl, xl)
                            for z in reversed(range(Z))
                            for y in (4 + yl, 6 + yl, yl, 2 + yl)
                        ]
                    )
    return groups


def finish_kernel(
    holders_ref, nodes_ref, own_ref, states_ref, params_ref, moment_ref, variance_ref, parity_ref,
    total_ref, sems,
):
    rows = params_ref.shape[0]
    copies = [
        pltpu.make_async_copy(own_ref.at[pl.ds(rows * k, rows)], out_ref, sems.at[k])
        for k, out_ref in enumerate((params_ref, moment_ref, variance_ref))
    ]
    for copy in copies:
        copy.start()
    member = lax.axis_index(CODE)
    holders = holders_ref[...]
    nodes = nodes_ref[...].astype(jnp.float32)
    total = None
    for i in range(states_ref.shape[0]):
        weight = jnp.zeros((1, 1), jnp.float32)
        for j in range(2):
            held = jnp.where(holders[:, j : j + 1] == member, 4.0, 0.0)
            weight += held / (nodes[:, j : j + 1] + nodes[:, 2 + i : 3 + i])
        term = weight * states_ref[i]
        total = term if total is None else total + term
    total_ref[...] = total
    copies.append(pltpu.make_async_copy(total_ref, parity_ref, sems.at[3]))
    copies[3].start()
    for copy in copies:
        copy.wait()


def local(grad_parts, params, moment, variance, holders, nodes):
    width = params.shape[2]
    rows = width // LANES

    parts = grad_parts.reshape(X // 2, 2, Z, Y // 2, 2, rows, LANES)
    parts = parts.transpose(1, 4, 0, 2, 3, 5, 6).reshape(4, X * Z * Y // 4, rows, LANES)
    parts = lax.all_to_all(
        parts, DP + CODE, 0, 0, tiled=True, axis_index_groups=near_groups()
    )
    summed = jnp.sum(parts.astype(jnp.float32), axis=0)
    summed = (summed * SCALE).astype(jnp.float16)
    pieces = summed.reshape(X // 2, Z, 2, Y // 4, rows, LANES)
    pieces = lax.rev(pieces, (0, 1, 2)).reshape(summed.shape)
    summed = lax.all_to_all(
        pieces, DP + CODE, 0, 0, tiled=True, axis_index_groups=far_groups()
    )
    gradient = jnp.sum(summed.astype(jnp.float32), axis=0) * (1.0 / SCALE)

    gradient, params, moment, variance = lax.optimization_barrier(
        (
            gradient,
            params.reshape(rows, LANES),
            moment.reshape(rows, LANES),
            variance.reshape(rows, LANES),
        )
    )
    new_moment = beta_one * moment + (1.0 - beta_one) * gradient
    new_variance = beta_two * variance + (1.0 - beta_two) * gradient * gradient
    update = (
        new_moment / bias_one / (jnp.sqrt(new_variance / bias_two) + epsilon) + decay_rate * params
    )
    new_params = params - learn_rate * update

    own = jnp.concatenate([new_params, new_moment, new_variance], axis=0)
    states = lax.all_gather(own, CODE, axis=0, tiled=False)
    state = jax.ShapeDtypeStruct((rows, LANES), jnp.float32)
    new_params, new_moment, new_variance, parity = pl.pallas_call(
        finish_kernel,
        out_shape=(state, state, state, jax.ShapeDtypeStruct((3 * rows, LANES), jnp.float32)),
        in_specs=[pl.BlockSpec(memory_space=pltpu.VMEM)] * 4,
        out_specs=(pl.BlockSpec(memory_space=pl.ANY),) * 4,
        scratch_shapes=[
            pltpu.VMEM((3 * rows, LANES), jnp.float32),
            pltpu.SemaphoreType.DMA((4,)),
        ],
        compiler_params=pltpu.CompilerParams(vmem_limit_bytes=4 << 20),
    )(holders, nodes.reshape(1, -1), own, states)
    return (
        new_params.reshape(1, 1, width),
        new_moment.reshape(1, 1, width),
        new_variance.reshape(1, 1, width),
        parity.reshape(1, 1, 3, width),
    )


def solution(mesh):
    fine = Mesh(mesh.devices.reshape(X // 2, 2, Z, Y // 2, 2, 2, 2), DP + CODE)
    return jax.shard_map(
        local,
        mesh=fine,
        in_specs=(
            P(DP, CODE, None, None),
            P(CODE, DP, None),
            P(CODE, DP, None),
            P(CODE, DP, None),
            P(DP, None),
            P(),
        ),
        out_specs=(
            P(CODE, DP, None),
            P(CODE, DP, None),
            P(CODE, DP, None),
            P(CODE, DP, None, None),
        ),
        check_vma=False,
    )
```

```python
import jax
import jax.numpy as jnp
from jax import lax
from jax.experimental import pallas as pl
from jax.experimental.pallas import tpu as pltpu
from jax.sharding import Mesh, PartitionSpec as P

beta_one = 0.9
beta_two = 0.95
learn_rate = 0.02
decay_rate = 0.1
epsilon = 1e-08
bias_one = 1.0 - 0.9**60
bias_two = 1.0 - 0.95**60

X, Z, Y = 4, 4, 8
DP = ("xh", "xl", "zh", "yh", "yl")
CODE = ("zl", "core")
LANES = 128
SCALE = 4096.0
FIRST = 30


def pairs(size, shifted):
    return [((2 * k + 2 * shifted) % size, 2 * k + 1) for k in range(size // 2)]


def near_groups():
    groups = []
    for z in range(Z):
        for zl in range(2):
            for core in range(2):
                for along_x in pairs(X, core):
                    for along_y in pairs(Y, core):
                        groups.append(
                            [
                                (((x * Z + z) * Y + y) * 2 + zl) * 2 + core
                                for x in along_x
                                for y in along_y
                            ]
                        )
    return groups


def far_groups():
    groups = []
    for xl in range(2):
        for yl in range(2):
            for zl in range(2):
                for core in range(2):
                    group = [
                        (((x * Z + z) * Y + y) * 2 + zl) * 2 + core
                        for x in range(xl, X, 2)
                        for z in range(Z)
                        for y in range(yl, Y, 2)
                    ]
                    groups.append(group[FIRST:] + group[:FIRST])
    return groups


def finish_kernel(
    holders_ref, nodes_ref, own_ref, states_ref, params_ref, moment_ref, variance_ref, parity_ref,
    total_ref, sems,
):
    rows = params_ref.shape[0]
    copies = [
        pltpu.make_async_copy(own_ref.at[pl.ds(rows * k, rows)], out_ref, sems.at[k])
        for k, out_ref in enumerate((params_ref, moment_ref, variance_ref))
    ]
    for copy in copies:
        copy.start()
    member = lax.axis_index(CODE)
    holders = holders_ref[...]
    nodes = nodes_ref[...].astype(jnp.float32)
    total = None
    for i in range(states_ref.shape[0]):
        weight = jnp.zeros((1, 1), jnp.float32)
        for j in range(2):
            held = jnp.where(holders[:, j : j + 1] == member, 4.0, 0.0)
            weight += held / (nodes[:, j : j + 1] + nodes[:, 2 + i : 3 + i])
        term = weight * states_ref[i]
        total = term if total is None else total + term
    total_ref[...] = total
    copies.append(pltpu.make_async_copy(total_ref, parity_ref, sems.at[3]))
    copies[3].start()
    for copy in copies:
        copy.wait()


def local(grad_parts, params, moment, variance, holders, nodes):
    width = params.shape[2]
    rows = width // LANES

    parts = grad_parts.reshape(X // 2, 2, Z, Y // 2, 2, rows, LANES)
    parts = parts.transpose(1, 4, 0, 2, 3, 5, 6).reshape(4, X * Z * Y // 4, rows, LANES)
    parts = lax.all_to_all(
        parts, DP + CODE, 0, 0, tiled=True, axis_index_groups=near_groups()
    )
    parts = jnp.concatenate([parts[:, FIRST:], parts[:, :FIRST]], axis=1).astype(jnp.float32)
    summed = (parts[0] + parts[1]) + (parts[2] + parts[3])
    summed = (summed * SCALE).astype(jnp.float16)
    summed = lax.all_to_all(
        summed, DP + CODE, 0, 0, tiled=True, axis_index_groups=far_groups()
    )
    gradient = jnp.sum(summed.astype(jnp.float32), axis=0) * (1.0 / SCALE)

    gradient, params, moment, variance = lax.optimization_barrier(
        (
            gradient,
            params.reshape(rows, LANES),
            moment.reshape(rows, LANES),
            variance.reshape(rows, LANES),
        )
    )
    new_moment = beta_one * moment + (1.0 - beta_one) * gradient
    new_variance = beta_two * variance + (1.0 - beta_two) * gradient * gradient
    update = (
        new_moment / bias_one / (jnp.sqrt(new_variance / bias_two) + epsilon) + decay_rate * params
    )
    new_params = params - learn_rate * update

    own = jnp.concatenate([new_params, new_moment, new_variance], axis=0)
    states = lax.all_gather(own, CODE, axis=0, tiled=False)
    state = jax.ShapeDtypeStruct((rows, LANES), jnp.float32)
    new_params, new_moment, new_variance, parity = pl.pallas_call(
        finish_kernel,
        out_shape=(state, state, state, jax.ShapeDtypeStruct((3 * rows, LANES), jnp.float32)),
        in_specs=[pl.BlockSpec(memory_space=pltpu.VMEM)] * 4,
        out_specs=(pl.BlockSpec(memory_space=pl.ANY),) * 4,
        scratch_shapes=[
            pltpu.VMEM((3 * rows, LANES), jnp.float32),
            pltpu.SemaphoreType.DMA((4,)),
        ],
        compiler_params=pltpu.CompilerParams(vmem_limit_bytes=4 << 20),
    )(holders, nodes.reshape(1, -1), own, states)
    return (
        new_params.reshape(1, 1, width),
        new_moment.reshape(1, 1, width),
        new_variance.reshape(1, 1, width),
        parity.reshape(1, 1, 3, width),
    )


def solution(mesh):
    fine = Mesh(mesh.devices.reshape(X // 2, 2, Z, Y // 2, 2, 2, 2), DP + CODE)
    return jax.shard_map(
        local,
        mesh=fine,
        in_specs=(
            P(DP, CODE, None, None),
            P(CODE, DP, None),
            P(CODE, DP, None),
            P(CODE, DP, None),
            P(DP, None),
            P(),
        ),
        out_specs=(
            P(CODE, DP, None),
            P(CODE, DP, None),
            P(CODE, DP, None),
            P(CODE, DP, None, None),
        ),
        check_vma=False,
    )
```

```python
import jax
import jax.numpy as jnp
from jax import lax
from jax.experimental import pallas as pl
from jax.experimental.pallas import tpu as pltpu
from jax.sharding import Mesh, PartitionSpec as P

beta_one = 0.9
beta_two = 0.95
learn_rate = 0.02
decay_rate = 0.1
epsilon = 1e-08
bias_one = 1.0 - 0.9**60
bias_two = 1.0 - 0.95**60

X, Z, Y = 4, 4, 8
DP = ("xh", "xl", "zh", "yh", "yl")
CODE = ("zl", "core")
LANES = 128
SCALE = 4096.0
FIRST = 30
MEMBERS = (2, 3, 0, 1)


def pairs(size, shifted):
    return [((2 * k + 2 * shifted) % size, 2 * k + 1) for k in range(size // 2)]


def near_groups():
    groups = []
    for z in range(Z):
        for zl in range(2):
            for core in range(2):
                for along_x in pairs(X, core):
                    for along_y in pairs(Y, core):
                        groups.append(
                            [
                                (((x * Z + z) * Y + y) * 2 + zl) * 2 + core
                                for x in along_x
                                for y in along_y
                            ]
                        )
    return groups


def far_groups():
    groups = []
    for xl in range(2):
        for yl in range(2):
            for zl in range(2):
                for core in range(2):
                    group = [
                        (((x * Z + z) * Y + y) * 2 + zl) * 2 + core
                        for x in range(xl, X, 2)
                        for z in range(Z)
                        for y in range(yl, Y, 2)
                    ]
                    groups.append(group[FIRST:] + group[:FIRST])
    return groups


def finish_kernel(
    holders_ref, nodes_ref, own_ref, states_ref, params_ref, moment_ref, variance_ref, parity_ref,
    total_ref, sems,
):
    rows = params_ref.shape[0]
    copies = [
        pltpu.make_async_copy(own_ref.at[pl.ds(rows * k, rows)], out_ref, sems.at[k])
        for k, out_ref in enumerate((params_ref, moment_ref, variance_ref))
    ]
    for copy in copies:
        copy.start()
    member = lax.axis_index(CODE)
    holders = holders_ref[...]
    nodes = nodes_ref[...].astype(jnp.float32)
    total = None
    for place, i in enumerate(MEMBERS):
        weight = jnp.zeros((1, 1), jnp.float32)
        for j in range(2):
            held = jnp.where(holders[:, j : j + 1] == member, 4.0, 0.0)
            weight += held / (nodes[:, j : j + 1] + nodes[:, 2 + i : 3 + i])
        term = weight * states_ref[place]
        total = term if total is None else total + term
    total_ref[...] = total
    copies.append(pltpu.make_async_copy(total_ref, parity_ref, sems.at[3]))
    copies[3].start()
    for copy in copies:
        copy.wait()


def local(grad_parts, params, moment, variance, holders, nodes):
    width = params.shape[2]
    rows = width // LANES

    parts = grad_parts.reshape(X // 2, 2, Z, Y // 2, 2, rows, LANES)
    parts = parts.transpose(1, 4, 0, 2, 3, 5, 6).reshape(4, X * Z * Y // 4, rows, LANES)
    parts = lax.all_to_all(
        parts, DP + CODE, 0, 0, tiled=True, axis_index_groups=near_groups()
    )
    parts = jnp.concatenate([parts[:, FIRST:], parts[:, :FIRST]], axis=1).astype(jnp.float32)
    summed = (parts[0] + parts[1]) + (parts[2] + parts[3])
    summed = (summed * SCALE).astype(jnp.float16)
    summed = lax.all_to_all(
        summed, DP + CODE, 0, 0, tiled=True, axis_index_groups=far_groups()
    )
    gradient = jnp.sum(summed.astype(jnp.float32), axis=0) * (1.0 / SCALE)

    gradient, params, moment, variance = lax.optimization_barrier(
        (
            gradient,
            params.reshape(rows, LANES),
            moment.reshape(rows, LANES),
            variance.reshape(rows, LANES),
        )
    )
    new_moment = beta_one * moment + (1.0 - beta_one) * gradient
    new_variance = beta_two * variance + (1.0 - beta_two) * gradient * gradient
    update = (
        new_moment / bias_one / (jnp.sqrt(new_variance / bias_two) + epsilon) + decay_rate * params
    )
    new_params = params - learn_rate * update

    own = jnp.concatenate([new_params, new_moment, new_variance], axis=0)
    code_groups = [[4 * shard + i for i in MEMBERS] for shard in range(X * Z * Y)]
    states = lax.all_gather(
        own, DP + CODE, axis=0, tiled=False, axis_index_groups=code_groups
    )
    state = jax.ShapeDtypeStruct((rows, LANES), jnp.float32)
    new_params, new_moment, new_variance, parity = pl.pallas_call(
        finish_kernel,
        out_shape=(state, state, state, jax.ShapeDtypeStruct((3 * rows, LANES), jnp.float32)),
        in_specs=[pl.BlockSpec(memory_space=pltpu.VMEM)] * 4,
        out_specs=(pl.BlockSpec(memory_space=pl.ANY),) * 4,
        scratch_shapes=[
            pltpu.VMEM((3 * rows, LANES), jnp.float32),
            pltpu.SemaphoreType.DMA((4,)),
        ],
        compiler_params=pltpu.CompilerParams(vmem_limit_bytes=4 << 20),
    )(holders, nodes.reshape(1, -1), own, states)
    return (
        new_params.reshape(1, 1, width),
        new_moment.reshape(1, 1, width),
        new_variance.reshape(1, 1, width),
        parity.reshape(1, 1, 3, width),
    )


def solution(mesh):
    fine = Mesh(mesh.devices.reshape(X // 2, 2, Z, Y // 2, 2, 2, 2), DP + CODE)
    return jax.shard_map(
        local,
        mesh=fine,
        in_specs=(
            P(DP, CODE, None, None),
            P(CODE, DP, None),
            P(CODE, DP, None),
            P(CODE, DP, None),
            P(DP, None),
            P(),
        ),
        out_specs=(
            P(CODE, DP, None),
            P(CODE, DP, None),
            P(CODE, DP, None),
            P(CODE, DP, None, None),
        ),
        check_vma=False,
    )
```

```python
import jax
import jax.numpy as jnp
from jax import lax
from jax.experimental import pallas as pl
from jax.experimental.pallas import tpu as pltpu
from jax.sharding import Mesh, PartitionSpec as P

beta_one = 0.9
beta_two = 0.95
learn_rate = 0.02
decay_rate = 0.1
epsilon = 1e-08
bias_one = 1.0 - 0.9**60
bias_two = 1.0 - 0.95**60

X, Z, Y = 4, 4, 8
DP = ("xh", "xl", "zh", "yh", "yl")
CODE = ("zl", "core")
LANES = 128
SCALE = 4096.0
FIRST = 30


def pairs(size, shifted):
    return [((2 * k + 2 * shifted) % size, 2 * k + 1) for k in range(size // 2)]


def near_groups():
    groups = []
    for z in range(Z):
        for zl in range(2):
            for core in range(2):
                for along_x in pairs(X, core):
                    for along_y in pairs(Y, core):
                        groups.append(
                            [
                                (((x * Z + z) * Y + y) * 2 + zl) * 2 + core
                                for x in along_x
                                for y in along_y
                            ]
                        )
    return groups


def far_groups():
    groups = []
    for xl in range(2):
        for yl in range(2):
            for zl in range(2):
                for core in range(2):
                    group = [
                        (((x * Z + z) * Y + y) * 2 + zl) * 2 + core
                        for x in range(xl, X, 2)
                        for z in range(Z)
                        for y in range(yl, Y, 2)
                    ]
                    groups.append(group[FIRST:] + group[:FIRST])
    return groups


def finish_kernel(
    holders_ref, nodes_ref, own_ref, states_ref, params_ref, moment_ref, variance_ref, parity_ref,
    total_ref, sems,
):
    rows = params_ref.shape[0]
    copies = [
        pltpu.make_async_copy(own_ref.at[pl.ds(rows * k, rows)], out_ref, sems.at[k])
        for k, out_ref in enumerate((params_ref, moment_ref, variance_ref))
    ]
    for copy in copies:
        copy.start()
    member = lax.axis_index(CODE)
    holders = holders_ref[...]
    nodes = nodes_ref[...].astype(jnp.float32)
    total = None
    for i in range(states_ref.shape[0]):
        weight = jnp.zeros((1, 1), jnp.float32)
        for j in range(2):
            held = jnp.where(holders[:, j : j + 1] == member, 4.0, 0.0)
            weight += held / (nodes[:, j : j + 1] + nodes[:, 2 + i : 3 + i])
        term = weight * states_ref[i]
        total = term if total is None else total + term
    total_ref[...] = total
    copies.append(pltpu.make_async_copy(total_ref, parity_ref, sems.at[3]))
    copies[3].start()
    for copy in copies:
        copy.wait()


def local(grad_parts, params, moment, variance, holders, nodes):
    width = params.shape[2]
    rows = width // LANES

    parts = grad_parts.reshape(X // 2, 2, Z, Y // 2, 2, rows, LANES)
    parts = parts.transpose(1, 4, 0, 2, 3, 5, 6).reshape(4, X * Z * Y // 4, rows, LANES)
    parts = lax.all_to_all(
        parts, DP + CODE, 0, 0, tiled=True, axis_index_groups=near_groups()
    )
    summed = jnp.sum(parts.astype(jnp.float32), axis=0) * SCALE
    summed = jnp.concatenate([summed[FIRST:], summed[:FIRST]], axis=0).astype(jnp.float16)
    summed = lax.all_to_all(
        summed, DP + CODE, 0, 0, tiled=True, axis_index_groups=far_groups()
    )
    gradient = jnp.sum(summed.astype(jnp.float32), axis=0) * (1.0 / SCALE)

    gradient, params, moment, variance = lax.optimization_barrier(
        (
            gradient,
            params.reshape(rows, LANES),
            moment.reshape(rows, LANES),
            variance.reshape(rows, LANES),
        )
    )
    new_moment = beta_one * moment + (1.0 - beta_one) * gradient
    new_variance = beta_two * variance + (1.0 - beta_two) * gradient * gradient
    update = (
        new_moment / bias_one / (jnp.sqrt(new_variance / bias_two) + epsilon) + decay_rate * params
    )
    new_params = params - learn_rate * update

    own = jnp.concatenate([new_params, new_moment, new_variance], axis=0)
    states = lax.all_gather(own, CODE, axis=0, tiled=False)
    state = jax.ShapeDtypeStruct((rows, LANES), jnp.float32)
    new_params, new_moment, new_variance, parity = pl.pallas_call(
        finish_kernel,
        out_shape=(state, state, state, jax.ShapeDtypeStruct((3 * rows, LANES), jnp.float32)),
        in_specs=[pl.BlockSpec(memory_space=pltpu.VMEM)] * 4,
        out_specs=(pl.BlockSpec(memory_space=pl.ANY),) * 4,
        scratch_shapes=[
            pltpu.VMEM((3 * rows, LANES), jnp.float32),
            pltpu.SemaphoreType.DMA((4,)),
        ],
        compiler_params=pltpu.CompilerParams(vmem_limit_bytes=4 << 20),
    )(holders, nodes.reshape(1, -1), own, states)
    return (
        new_params.reshape(1, 1, width),
        new_moment.reshape(1, 1, width),
        new_variance.reshape(1, 1, width),
        parity.reshape(1, 1, 3, width),
    )


def solution(mesh):
    fine = Mesh(mesh.devices.reshape(X // 2, 2, Z, Y // 2, 2, 2, 2), DP + CODE)
    return jax.shard_map(
        local,
        mesh=fine,
        in_specs=(
            P(DP, CODE, None, None),
            P(CODE, DP, None),
            P(CODE, DP, None),
            P(CODE, DP, None),
            P(DP, None),
            P(),
        ),
        out_specs=(
            P(CODE, DP, None),
            P(CODE, DP, None),
            P(CODE, DP, None),
            P(CODE, DP, None, None),
        ),
        check_vma=False,
    )
```
